32 devices in a mesh: groups: 2 (over y), replica: 4 (over z), tensor: 2 (over x), sub: 2 (over core).
Axes of the slice: x: 2, y: 2, z: 4, core: 2. Of those that a mesh axis runs over, the one named last changes fastest.
Arguments:
- activations: bfloat16 [6144, 4096], P(('groups', 'replica', 'sub'), 'tensor'), parts along dimension 0, may hold values from -6 to 6
- row_voice_index: int32 [6144], P(('groups', 'replica', 'sub')), parts along dimension 0, may hold values from 0 to 51, as said below
- voice_slot_table: int32 [104], P('groups'), parts along dimension 0, may hold values from 0 to 51, as said below
- value_weight_matrix: bfloat16 [4096, 1024], P('tensor'), may hold values from -0.09375 to 0.09375
- adapter_down_weight: bfloat16 [104, 16, 4096], P(('groups', 'replica'), None, 'tensor'), parts along dimension 0, may hold values from -0.09375 to 0.09375
- adapter_up_weight: bfloat16 [104, 16, 1024], P(('groups', 'replica'), None, 'tensor'), parts along dimension 0, may hold values from -0.75 to 0.75
Outputs:
- values: bfloat16 [6144, 1024], P(('groups', 'replica', 'sub')), parts along dimension 0
The draws below stay inside these ranges and needn't reach their ends.
There are 2 independent parts, one for each index of `groups`. The reference program is written for one: setup_inputs(seed, part) draws one part's arguments, and reference() takes and returns one part's arrays. A program takes and returns all parts, laid end to end along the dimension named above; an argument that names none is the same for every part. Nothing has to cross between parts.
Inputs may be any that keep to these rules, and one draw needn't show every extreme that they name: Every slot is named by exactly one voice; voice v's panels are row voice_slot_table[v] of adapter_down_weight and adapter_up_weight, and its owner is voice_slot_table[v] // 13. `row_voice_index`: in each aligned block of 384 rows (the rows of one device) at most 96 rows name voices of any one owner, and exactly 96 rows name voices of one owner.
All inputs are finite; a program needn't handle non-finite values.
Results may differ from the reference program's by a relative error of at most 0.004.
Values may be sent and summed in bfloat16 or wider, within the bound.
A program may use at most 64 MiB of HBM per device.

```python
import jax
import jax.numpy as jnp
from jax import lax

MODEL_WIDTH = 4096
VALUE_WIDTH = 1024
ADAPTER_RANK = 16
VOICE_DEV = 13
ROWS_DEV = 384
VOICE_COUNT = 52
CAP = 96
ROWS = 3072


def shared_slots(key):
    return jax.random.permutation(key, VOICE_COUNT).astype(jnp.int32)


def draw_voice_slot_table(key, part):
    placed = shared_slots(key)
    return placed


def draw_row_voice_index(key, part):
    placed = shared_slots(key)
    key = jax.random.fold_in(key, 11)
    owner_count = VOICE_COUNT // VOICE_DEV
    block_count = ROWS // ROWS_DEV
    key_hot, key_alt, key_order, key_shift, key_voice = jax.random.split(key, 5)
    hot_owner = jnp.minimum(jax.random.randint(key_hot, (block_count, 1), 0, owner_count), jax.random.randint(key_alt, (block_count, 1), 0, owner_count))
    row_order = jax.vmap(lambda sub_key: jax.random.permutation(sub_key, ROWS_DEV))(jax.random.split(key_order, block_count))
    others = max(owner_count - 1, 1)
    offset = jax.random.randint(key_shift, (block_count, 1), 0, others)
    spread_rank = (row_order - CAP + offset) % others
    holder_position = jnp.where(row_order < CAP, hot_owner, (hot_owner + 1 + spread_rank) % owner_count)
    within = jax.random.randint(key_voice, (block_count, ROWS_DEV), 0, VOICE_DEV)
    slot_index = holder_position * VOICE_DEV + within
    inverse = jnp.zeros((VOICE_COUNT,), jnp.int32).at[placed].set(jnp.arange(VOICE_COUNT, dtype=jnp.int32))
    return inverse[slot_index].reshape(ROWS).astype(jnp.int32)


def steps_of(own_key, shape, pieces, low, top_value):
    level, own = 1.0, jax.random.fold_in(own_key, 6)
    for position, shards_of in pieces:
        heights = jnp.exp(jax.random.uniform(jax.random.fold_in(own, position), (shards_of,), jnp.float32, low / len(pieces), top_value / len(pieces)))
        level = level * jnp.repeat(heights, shape[position] // shards_of).reshape([-1 if axis == position else 1 for axis in range(len(shape))])
    return level


def scatter_about(rng, shape, deviation, most, shards=(), kind=jnp.bfloat16):
    level = steps_of(rng, shape, shards, -0.22, 0.18) if shards else 1.0
    result = jax.random.normal(rng, shape, jnp.float32) * deviation * level
    return jnp.minimum(jnp.maximum(result, -most), most).astype(kind)


def setup_inputs(seed: int = 0, part: int = 0) -> dict:
    keys = jax.random.split(jax.random.key(seed), 7)
    own_keys = jax.random.split(jax.random.fold_in(keys[6], part), 7)
    return {
        "activations": scatter_about(own_keys[0], (ROWS, MODEL_WIDTH), 1.0, 6.0, ((0, 8), (1, 2))),
        "row_voice_index": draw_row_voice_index(jax.random.fold_in(jax.random.fold_in(keys[6], part), 71), part),
        "voice_slot_table": draw_voice_slot_table(jax.random.fold_in(jax.random.fold_in(keys[6], part), 71), part),
        "value_weight_matrix": scatter_about(keys[3], (MODEL_WIDTH, VALUE_WIDTH), MODEL_WIDTH ** -0.5, 0.09375, ((0, 2),)),
        "adapter_down_weight": scatter_about(own_keys[4], (VOICE_COUNT, ADAPTER_RANK, MODEL_WIDTH), MODEL_WIDTH ** -0.5, 0.09375, ((0, 4), (2, 2))),
        "adapter_up_weight": scatter_about(own_keys[5], (VOICE_COUNT, ADAPTER_RANK, VALUE_WIDTH), (4 * ADAPTER_RANK) ** -0.5, 0.75, ((0, 4), (2, 2))),
    }


DELTA_GAIN = 2.0


def reference(activations, row_voice_index, voice_slot_table, value_weight_matrix, adapter_down_weight, adapter_up_weight):
    slot_of_row = jnp.take(voice_slot_table, row_voice_index).astype(jnp.int32)
    base_product = jnp.dot(activations, value_weight_matrix, preferred_element_type=jnp.float32)
    block_count = activations.shape[0] // ROWS_DEV
    activation_blocks = activations.reshape(block_count, ROWS_DEV, MODEL_WIDTH)
    slot_block_ids = slot_of_row.reshape(block_count, ROWS_DEV)

    def block_update(block_item):
        rows_per_block, row_slot_index = block_item
        down_matrices = jnp.take(adapter_down_weight, row_slot_index, axis=0).astype(jnp.float32)
        narrowed_hidden = jnp.einsum("lxa,la->lx", down_matrices, rows_per_block.astype(jnp.float32)).astype(jnp.bfloat16)
        expanding_factors = jnp.take(adapter_up_weight, row_slot_index, axis=0).astype(jnp.float32)
        return DELTA_GAIN * jnp.einsum("cl,cls->cs", narrowed_hidden.astype(jnp.float32), expanding_factors)

    speaker_correction = lax.map(block_update, (activation_blocks, slot_block_ids)).reshape(activations.shape[0], VALUE_WIDTH)
    return (base_product + speaker_correction).astype(jnp.bfloat16)
```

```python
import functools

import jax
import jax.numpy as jnp
from jax import lax
from jax.experimental import pallas as pl
from jax.experimental.pallas import tpu as pltpu
from jax.sharding import PartitionSpec as P

DELTA_GAIN = 2.0
MESH = pl.DeviceIdType.MESH
TILE = 256
F32 = jnp.float32
BF16 = jnp.bfloat16


def kernel(
    n,
    t,
    voices,
    rank,
    voice,
    table,
    act,
    weight,
    down,
    up,
    out,
    act_v,
    w_v,
    pd,
    pu,
    xb,
    total,
    xr,
    slot_v,
    z_send,
    z_recv,
    sib_send,
    sib_recv,
    xu_send,
    xu_recv,
    sx_send,
    sx_recv,
    xb_send,
    xb_recv,
    xr_send,
    xr_recv,
    w_sem,
    loc_sem,
):
    rows, feat = act_v.shape
    width = w_v.shape[1]
    span = up.shape[1]
    panel = voices * rank
    tiles = width // TILE
    me = lax.axis_index("replica")
    mx = lax.axis_index("tensor")
    core = lax.axis_index("sub")
    hu, hd, qd = span // 2, feat // 2, feat // 4

    def peer(p):
        return lax.rem(mx + p, t)

    def slab(o):
        return pl.ds(pl.multiple_of(o * panel, 16), panel)

    def u_cols(k):
        return pl.ds(pl.multiple_of(k * hu, 128), hu)

    def d_cols(k, j):
        return pl.ds(pl.multiple_of(k * hd + j * qd, 128), qd)

    def piece(o, j, k):
        if j == 0:
            return pu.at[mx, slab(o), u_cols(k)]
        return pd.at[o, :, d_cols(k, j - 1)]

    def own_piece(j):
        if j == 0:
            return up.at[:, u_cols(core)]
        return down.at[:, d_cols(core, j - 1)]

    def z_copy(direction, o, j, own=False):
        return pltpu.make_async_remote_copy(
            src_ref=own_piece(j) if own else piece(o, j, core),
            dst_ref=piece(o, j, core),
            send_sem=z_send.at[(direction + 1) // 2, o, j],
            recv_sem=z_recv.at[o, j],
            device_id={"replica": me + direction},
            device_id_type=MESH,
        )

    def sib_copy(o, j, k):
        return pltpu.make_async_remote_copy(
            src_ref=piece(o, j, k),
            dst_ref=piece(o, j, k),
            send_sem=sib_send.at[o, j],
            recv_sem=sib_recv.at[o, j],
            device_id={"sub": 1 - core},
            device_id_type=MESH,
        )

    def xu_copy(o, p, own=False):
        return pltpu.make_async_remote_copy(
            src_ref=own_piece(0) if own else piece(o, 0, core),
            dst_ref=piece(o, 0, core),
            send_sem=xu_send.at[o, p],
            recv_sem=xu_recv.at[o, t - p],
            device_id={"tensor": peer(p)},
            device_id_type=MESH,
        )

    def xu_arrival(o, p, k, send, recv):
        where = pu.at[peer(p), slab(o), u_cols(k)]
        return pltpu.make_async_remote_copy(
            src_ref=where,
            dst_ref=where,
            send_sem=send.at[o, p],
            recv_sem=recv.at[o, p],
            device_id={"sub": 1 - core},
            device_id_type=MESH,
        )

    def b_cols(i):
        return pl.ds(pl.multiple_of(i * TILE, TILE), TILE)

    def xb_copy(i, p, owner):
        return pltpu.make_async_remote_copy(
            src_ref=xb.at[owner, :, b_cols(i)],
            dst_ref=xb.at[owner, :, b_cols(i)],
            send_sem=xb_send.at[i, p],
            recv_sem=xb_recv.at[i, t - p],
            device_id={"tensor": peer(p)},
            device_id_type=MESH,
        )

    def xr_copy(s, p, owner):
        return pltpu.make_async_remote_copy(
            src_ref=xr.at[s, owner],
            dst_ref=xr.at[s, owner],
            send_sem=xr_send.at[s, p],
            recv_sem=xr_recv.at[s, t - p],
            device_id={"tensor": peer(p)},
            device_id_type=MESH,
        )

    def w_copy(i):
        return pltpu.make_async_copy(weight.at[:, b_cols(i)], w_v.at[:, b_cols(i)], w_sem.at[i])

    barrier = pltpu.get_barrier_semaphore()

    def greet(device):
        pl.semaphore_signal(barrier, inc=1, device_id=device, device_id_type=MESH)

    act_copy = pltpu.make_async_copy(act, act_v, loc_sem.at[0])
    down_copy = pltpu.make_async_copy(down, pd.at[me], loc_sem.at[1])
    up_copy = pltpu.make_async_copy(up, pu.at[mx, slab(me)], loc_sem.at[2])
    greet({"sub": 1 - core})
    for p in range(1, t):
        greet({"tensor": peer(p)})
    pl.when(me > 0)(lambda: greet({"replica": me - 1}))
    pl.when(me < n - 1)(lambda: greet({"replica": me + 1}))
    act_copy.start()
    for i in range(tiles):
        w_copy(i).start()
    down_copy.start()
    up_copy.start()
    ends = (me == 0).astype(jnp.int32) + (me == n - 1).astype(jnp.int32)
    pl.semaphore_wait(barrier, t + 2 - ends)

    for j in range(3):
        pl.when(me > 0)(lambda: z_copy(-1, me, j, True).start())
        pl.when(me < n - 1)(lambda: z_copy(1, me, j, True).start())
    for p in range(1, t):
        xu_copy(me, p, True).start()

    act_copy.wait()

    def base_tile(i, carry):
        w_copy(i).wait()
        part = jnp.dot(act_v[...], w_v[:, b_cols(i)], preferred_element_type=F32)
        xb[mx, :, b_cols(i)] = part.astype(BF16)
        for p in range(1, t):
            xb_copy(i, p, mx).start()
        return carry

    lax.fori_loop(0, tiles, base_tile, 0)

    row_voice = voice[...]

    def slot_step(v, slot):
        return jnp.where(row_voice == v, table[v], slot)

    slot_v[...] = lax.fori_loop(0, table.shape[0], slot_step, jnp.zeros_like(row_voice))

    def mask_of(o):
        section = lax.broadcasted_iota(jnp.int32, (panel, rows), 0) // rank
        return section == (slot_v[...] - o * voices)

    def project(o):
        made = lax.dot_general(
            pd[o], act_v[...], (((1,), (1,)), ((), ())), preferred_element_type=F32
        )
        kept = jnp.where(mask_of(o), made, 0.0)
        return kept.reshape(voices, rank, rows).sum(axis=0)

    def send_rank(s):
        for p in range(1, t):
            xr_copy(s, p, mx).start()

    def settle_owner(o, narrowed):
        for p in range(1, t):
            xu_arrival(o, p, core, xu_send, xu_recv).wait_recv()
            xu_arrival(o, p, core, sx_send, sx_recv).start()
        wide = jnp.where(mask_of(o), jnp.tile(narrowed, (voices, 1)), jnp.zeros((), BF16))
        for p in range(1, t):
            xu_arrival(o, p, 1 - core, sx_send, sx_recv).wait_recv()
        for x in range(t):
            total[:, x * span : (x + 1) * span] += lax.dot_general(
                wide, pu[x, slab(o)], (((0,), (0,)), ((), ())), preferred_element_type=F32
            )

    def rank_sum(s):
        for p in range(1, t):
            xr_copy(s, p, peer(p)).wait_recv()
        acc = xr[s, 0]
        for x in range(1, t):
            acc = acc + xr[s, x]
        return (DELTA_GAIN * acc.astype(BF16).astype(F32)).astype(BF16)

    def both(s, act_on):
        pl.when(me - s >= 0)(lambda: act_on(me - s, 1))
        pl.when(me + s < n)(lambda: act_on(me + s, -1))

    def settle(s):
        narrowed = rank_sum(s)
        both(s, lambda o, direction: settle_owner(o, narrowed))

    def onward(direction):
        return (me + direction >= 0) & (me + direction < n)

    total[...] = jnp.zeros_like(total)
    down_copy.wait()
    up_copy.wait()
    xr[0, mx] = project(me)
    send_rank(0)

    def step(s, carry):
        for j in range(3):

            def take(o, direction):
                z_copy(direction, o, j).wait_recv()
                pl.when(onward(direction))(lambda: z_copy(direction, o, j).start())
                sib_copy(o, j, core).start()
                if j == 0:
                    for p in range(1, t):
                        xu_copy(o, p).start()

            both(s, take)
        xr[s, mx] = jnp.zeros((rank, rows), F32)

        def work(o, direction):
            for j in range(3):
                sib_copy(o, j, 1 - core).wait_recv()
            xr[s, mx] += project(o)

        both(s, work)
        send_rank(s)

        @pl.when(s == 1)
        def _():
            settle_owner(me, rank_sum(0))

        @pl.when(s > 1)
        def _():
            settle(s - 1)

        return carry

    lax.fori_loop(1, n, step, 0)
    settle(n - 1)

    def base_wait(i, carry):
        for p in range(1, t):
            xb_copy(i, p, peer(p)).wait_recv()
        acc = total[:, b_cols(i)]
        for x in range(t):
            acc = acc + xb[x, :, b_cols(i)].astype(F32)
        out[:, b_cols(i)] = acc.astype(BF16)
        for p in range(1, t):
            xb_copy(i, p, mx).wait_send()
        return carry

    lax.fori_loop(0, tiles, base_wait, 0)

    for j in range(3):
        pl.when(me > 0)(lambda: z_copy(-1, me, j, True).wait_send())
        pl.when(me < n - 1)(lambda: z_copy(1, me, j, True).wait_send())
    for p in range(1, t):
        xu_copy(me, p, True).wait_send()
        xu_arrival(me, p, core, sx_send, sx_recv).wait_send()
        xr_copy(0, p, mx).wait_send()

    def drain(s, carry):
        def sent(o, direction):
            for j in range(3):
                pl.when(onward(direction))(lambda: z_copy(direction, o, j).wait_send())
                sib_copy(o, j, core).wait_send()
            for p in range(1, t):
                xu_copy(o, p).wait_send()
                xu_arrival(o, p, core, sx_send, sx_recv).wait_send()

        both(s, sent)
        for p in range(1, t):
            xr_copy(s, p, mx).wait_send()
        return carry

    lax.fori_loop(1, n, drain, 0)


def local(n, t, activations, row_voice, slot_table, weight, down, up):
    rows, feat = activations.shape
    voices, rank, span = up.shape
    width = weight.shape[1]
    panel = voices * rank
    any_spec = pl.BlockSpec(memory_space=pl.ANY)
    dma = pltpu.SemaphoreType.DMA
    return pl.pallas_call(
        functools.partial(kernel, n, t, voices, rank),
        out_shape=jax.ShapeDtypeStruct((rows, width), BF16),
        in_specs=[
            pl.BlockSpec(memory_space=pltpu.VMEM),
            pl.BlockSpec(memory_space=pltpu.SMEM),
            any_spec,
            any_spec,
            any_spec,
            any_spec,
        ],
        out_specs=pl.BlockSpec(memory_space=pltpu.VMEM),
        scratch_shapes=[
            pltpu.VMEM((rows, feat), BF16),
            pltpu.VMEM((feat, width), BF16),
            pltpu.VMEM((n, panel, feat), BF16),
            pltpu.VMEM((t, n * panel, span), BF16),
            pltpu.VMEM((t, rows, width), BF16),
            pltpu.VMEM((rows, width), F32),
            pltpu.VMEM((n, t, rank, rows), F32),
            pltpu.VMEM((1, rows), jnp.int32),
            dma((2, n, 3)),
            dma((n, 3)),
            dma((n, 3)),
            dma((n, 3)),
            dma((n, t)),
            dma((n, t)),
            dma((n, t)),
            dma((n, t)),
            dma((width // TILE, t)),
            dma((width // TILE, t)),
            dma((n, t)),
            dma((n, t)),
            dma((width // TILE,)),
            dma((3,)),
        ],
        compiler_params=pltpu.CompilerParams(
            collective_id=0, has_side_effects=True, vmem_limit_bytes=56 * 1024 * 1024
        ),
    )(
        row_voice.reshape(1, rows),
        slot_table,
        activations,
        weight,
        down.reshape(panel, feat),
        up.reshape(panel, span),
    )


def solution(mesh):
    in_specs = (
        P(("groups", "replica", "sub"), "tensor"),
        P(("groups", "replica", "sub")),
        P("groups"),
        P("tensor", None),
        P(("groups", "replica"), None, "tensor"),
        P(("groups", "replica"), None, "tensor"),
    )
    out_specs = P(("groups", "replica", "sub"), None)
    body = functools.partial(local, mesh.shape["replica"], mesh.shape["tensor"])
    return jax.shard_map(body, mesh=mesh, in_specs=in_specs, out_specs=out_specs, check_vma=False)
```

```python
import functools

import jax
import jax.numpy as jnp
from jax import lax
from jax.experimental import pallas as pl
from jax.experimental.pallas import tpu as pltpu
from jax.sharding import PartitionSpec as P

DELTA_GAIN = 2.0
MESH = pl.DeviceIdType.MESH
TILE = 256
PARTS = 4
F32 = jnp.float32
BF16 = jnp.bfloat16


def kernel(
    n,
    t,
    voices,
    rank,
    cap,
    voice,
    table,
    act,
    weight,
    down,
    up,
    out,
    act_v,
    w_v,
    pd,
    pu,
    xb,
    total,
    xr,
    slot_v,
    made_v,
    perm_v,
    rows_out,
    tags_out,
    rows_in,
    tags_in,
    back_out,
    back_in,
    z_send,
    z_recv,
    sib_send,
    sib_recv,
    xu_send,
    xu_recv,
    sx_send,
    sx_recv,
    xb_send,
    xb_recv,
    xr_send,
    xr_recv,
    w_sem,
    loc_sem,
    trade_send,
    trade_recv,
):
    rows, feat = act_v.shape
    width = w_v.shape[1]
    span = up.shape[1]
    panel = voices * rank
    tile = min(TILE, span)
    tiles = width // tile
    me = lax.axis_index("replica")
    mx = lax.axis_index("tensor")
    core = lax.axis_index("sub")
    hu, hd, qd = span // 2, feat // 2, feat // (2 * PARTS)
    pieces = PARTS + 1
    trade = n >= 4
    is_end = ((me == 0) | (me == n - 1)) if trade else (me < 0)
    is_host = ((me == 1) | (me == n - 2)) if trade else (me < 0)
    inward = jnp.where(me == 0, 1, -1)
    outward = jnp.where(me == 1, -1, 1)
    lanes = perm_v.shape[0]

    def peer(p):
        return lax.rem(mx + p, t)

    def slab(o):
        return pl.ds(pl.multiple_of(o * panel, 16), panel)

    def u_cols(k):
        return pl.ds(pl.multiple_of(k * hu, 128), hu)

    def d_cols(k, j):
        return pl.ds(pl.multiple_of(k * hd + (j - 1) * qd, 128), qd)

    def piece(o, j, k):
        if j == 0:
            return pu.at[mx, slab(o), u_cols(k)]
        return pd.at[o, :, d_cols(k, j)]

    def own_piece(j):
        if j == 0:
            return up.at[:, u_cols(core)]
        return down.at[:, d_cols(core, j)]

    def z_copy(direction, o, j, own=False):
        return pltpu.make_async_remote_copy(
            src_ref=own_piece(j) if own else piece(o, j, core),
            dst_ref=piece(o, j, core),
            send_sem=z_send.at[(direction + 1) // 2, o, j],
            recv_sem=z_recv.at[o, j],
            device_id={"replica": me + direction},
            device_id_type=MESH,
        )

    def sib_copy(o, j, k):
        return pltpu.make_async_remote_copy(
            src_ref=piece(o, j, k),
            dst_ref=piece(o, j, k),
            send_sem=sib_send.at[o, j],
            recv_sem=sib_recv.at[o, j],
            device_id={"sub": 1 - core},
            device_id_type=MESH,
        )

    def xu_copy(o, p):
        return pltpu.make_async_remote_copy(
            src_ref=piece(o, 0, core),
            dst_ref=piece(o, 0, core),
            send_sem=xu_send.at[o, p],
            recv_sem=xu_recv.at[o, t - p],
            device_id={"tensor": peer(p)},
            device_id_type=MESH,
        )

    def xu_arrival(o, p, k, send, recv):
        where = pu.at[peer(p), slab(o), u_cols(k)]
        return pltpu.make_async_remote_copy(
            src_ref=where,
            dst_ref=where,
            send_sem=send.at[o, p],
            recv_sem=recv.at[o, p],
            device_id={"sub": 1 - core},
            device_id_type=MESH,
        )

    def b_cols(i):
        return pl.ds(pl.multiple_of(i * tile, 128), tile)

    def xb_copy(i, p, owner):
        return pltpu.make_async_remote_copy(
            src_ref=xb.at[owner, :, b_cols(i)],
            dst_ref=xb.at[owner, :, b_cols(i)],
            send_sem=xb_send.at[i, p],
            recv_sem=xb_recv.at[i, t - p],
            device_id={"tensor": peer(p)},
            device_id_type=MESH,
        )

    def xr_copy(s, p, owner):
        return pltpu.make_async_remote_copy(
            src_ref=xr.at[s, owner],
            dst_ref=xr.at[s, owner],
            send_sem=xr_send.at[s, p],
            recv_sem=xr_recv.at[s, t - p],
            device_id={"tensor": peer(p)},
            device_id_type=MESH,
        )

    def trade_copy(k, src, dst, direction):
        return pltpu.make_async_remote_copy(
            src_ref=src,
            dst_ref=dst,
            send_sem=trade_send.at[k],
            recv_sem=trade_recv.at[k],
            device_id={"replica": me + direction},
            device_id_type=MESH,
        )

    def rows_copy():
        return trade_copy(0, rows_out, rows_in.at[pl.ds(0, rows_out.shape[0])], inward)

    def tags_copy():
        return trade_copy(1, tags_out, tags_in, inward)

    def back_copy():
        return trade_copy(2, back_out, back_in, outward)

    def w_copy(i):
        return pltpu.make_async_copy(weight.at[:, b_cols(i)], w_v.at[:, b_cols(i)], w_sem.at[i])

    barrier = pltpu.get_barrier_semaphore()

    def greet(device):
        pl.semaphore_signal(barrier, inc=1, device_id=device, device_id_type=MESH)

    act_copy = pltpu.make_async_copy(act, act_v, loc_sem.at[0])
    down_copy = pltpu.make_async_copy(down, pd.at[me], loc_sem.at[1])
    up_copy = pltpu.make_async_copy(up, pu.at[mx, slab(me)], loc_sem.at[2])
    greet({"sub": 1 - core})
    for p in range(1, t):
        greet({"tensor": peer(p)})
    pl.when(me > 0)(lambda: greet({"replica": me - 1}))
    pl.when(me < n - 1)(lambda: greet({"replica": me + 1}))
    act_copy.start()
    down_copy.start()
    up_copy.start()
    order = [lax.rem((mx + 1) * (span // tile) + i, tiles) for i in range(tiles)]
    for i in order:
        w_copy(i).start()
    ends = (me == 0).astype(jnp.int32) + (me == n - 1).astype(jnp.int32)
    pl.semaphore_wait(barrier, t + 2 - ends)

    def on_line(o):
        return (o >= 0) & (o < n)

    def own_send(direction, j, act_on):
        to = me + direction
        wanted = on_line(to)
        if trade and j > 0:
            wanted = wanted & (to > 0) & (to < n - 1)
        pl.when(wanted)(lambda: act_on(z_copy(direction, me, j, True)))

    def own_sends(js, act_on):
        for j in js:
            for direction in (-1, 1):
                own_send(direction, j, act_on)

    early = 1 + PARTS // 2
    own_sends(range(early), lambda c: c.start())
    pl.when(jnp.logical_not(is_end))(
        lambda: own_sends(range(early, pieces), lambda c: c.start())
    )

    act_copy.wait()

    row_voice = voice[...]

    def slot_step(v, slot):
        return jnp.where(row_voice == v, table[v], slot)

    slot_v[...] = lax.fori_loop(0, table.shape[0], slot_step, jnp.zeros_like(row_voice))
    section = lax.broadcasted_iota(jnp.int32, (panel, rows), 0) // rank

    def mask_of(o):
        return section == (slot_v[...] - o * voices)

    def fold(kept):
        return kept.reshape(voices, rank, kept.shape[1]).sum(axis=0)

    def nt_dot(a, b):
        return lax.dot_general(a, b, (((1,), (1,)), ((), ())), preferred_element_type=F32)

    def tn_dot(a, b):
        return lax.dot_general(a, b, (((0,), (0,)), ((), ())), preferred_element_type=F32)

    def send_rank(s):
        for p in range(1, t):
            xr_copy(s, p, mx).start()

    def rank_sum(s):
        for p in range(1, t):
            xr_copy(s, p, peer(p)).wait_recv()
        acc = xr[s, 0]
        for x in range(1, t):
            acc = acc + xr[s, x]
        return (DELTA_GAIN * acc.astype(BF16).astype(F32)).astype(BF16)

    def widen(o, narrowed):
        return jnp.where(mask_of(o), jnp.tile(narrowed, (voices, 1)), jnp.zeros((), BF16))

    def both(s, act_on):
        pl.when(me - s >= 0)(lambda: act_on(me - s, 1))
        pl.when(me + s < n)(lambda: act_on(me + s, -1))

    def take(s, j):
        def one(o, direction):
            z_copy(direction, o, j).wait_recv()
            pl.when(on_line(me + direction))(lambda: z_copy(direction, o, j).start())
            sib_copy(o, j, core).start()
            if j == 0:
                for p in range(1, t):
                    xu_copy(o, p).start()

        both(s, one)

    def process(s, j):
        def one(o, direction):
            side = (direction + 1) // 2
            sib_copy(o, j, 1 - core).wait_recv()
            got = nt_dot(pd[o, :, d_cols(0, j)], act_v[:, d_cols(0, j)])
            got = got + nt_dot(pd[o, :, d_cols(1, j)], act_v[:, d_cols(1, j)])
            if j > 1:
                got = got + made_v[side]
            if j < PARTS:
                made_v[side] = got
            else:
                xr[s, mx] += fold(jnp.where(mask_of(o), got, 0.0))

        both(s, one)

    def relay(o):
        for p in range(1, t):
            xu_arrival(o, p, core, xu_send, xu_recv).wait_recv()
            xu_arrival(o, p, core, sx_send, sx_recv).start()

    def settle_owner(o, narrowed):
        wide = widen(o, narrowed)
        sib_copy(o, 0, 1 - core).wait_recv()
        for p in range(1, t):
            xu_arrival(o, p, 1 - core, sx_send, sx_recv).wait_recv()
        for x in range(t):
            total[:, x * span : (x + 1) * span] += tn_dot(wide, pu[x, slab(o)])

    def settle(s):
        both(s, lambda o, direction: relay(o))
        if trade:
            pl.when(is_end & (s == 2))(lambda: relay(me + inward))
        narrowed = rank_sum(s)
        both(s, lambda o, direction: settle_owner(o, narrowed))
        if trade:
            pl.when(is_end & (s == 2))(lambda: settle_owner(me + inward, narrowed))

    def busy(s):
        some = on_line(me - s) | on_line(me + s)
        if trade:
            some = some & jnp.logical_not(is_end & (s == 1))
        return some

    down_copy.wait()
    xr[0, mx] = fold(jnp.where(mask_of(me), nt_dot(pd[me], act_v[...]), 0.0))
    send_rank(0)
    up_copy.wait()

    def base_tile(i, extra=None):
        w_copy(i).wait()
        part = jnp.dot(act_v[...], w_v[:, b_cols(i)], preferred_element_type=F32)
        if extra is not None:
            part = part + extra
        xb[mx, :, b_cols(i)] = part.astype(BF16)
        for p in range(1, t):
            xb_copy(i, p, mx).start()

    def early_take(j):
        if j == 0 or not trade:
            take(1, j)
        else:
            pl.when(jnp.logical_not(is_end))(lambda: take(1, j))

    others = tiles - span // tile
    for k in range(others):
        base_tile(order[k])
        early_take(k)

    if trade:

        @pl.when(is_end)
        def _():
            target = me + inward
            local_slot = slot_v[...] - target * voices
            chosen = (local_slot >= 0) & (local_slot < voices)
            ones = chosen.astype(F32)
            up_to = lax.broadcasted_iota(jnp.int32, (rows, rows), 0) <= lax.broadcasted_iota(
                jnp.int32, (rows, rows), 1
            )
            counted = jnp.dot(
                jnp.broadcast_to(ones, (8, rows)).astype(BF16),
                up_to.astype(F32).astype(BF16),
                preferred_element_type=F32,
            )[0:1]
            place = lax.broadcasted_iota(jnp.int32, (lanes, rows), 0).astype(F32) + 1.0
            perm = jnp.where((place == counted) & chosen, 1.0, 0.0)
            perm_v[...] = perm
            picked = perm.astype(BF16)
            rows_out[...] = jnp.dot(
                picked[: rows_out.shape[0]], act_v[...], preferred_element_type=F32
            ).astype(BF16)
            tag = jnp.where(chosen, local_slot + 1, 0).astype(F32)
            tags_out[...] = nt_dot(jnp.broadcast_to(tag, (8, rows)).astype(BF16), picked)
            tags_copy().start()
            rows_copy().start()
            own_sends(range(early, pieces), lambda c: c.start())

    wide0 = widen(me, rank_sum(0))
    per = span // tile
    for k in range(per):
        cols = pl.ds(k * tile, tile)
        base_tile(order[others + k], tn_dot(wide0, pu[mx, slab(me), cols]))
        if others + k < pieces:
            early_take(others + k)
    for j in range(tiles, pieces):
        early_take(j)
    total[...] = jnp.zeros_like(total)

    @pl.when(busy(1))
    def _():
        xr[1, mx] = jnp.zeros((rank, rows), F32)
        for j in range(1, pieces):
            process(1, j)
        send_rank(1)

    def serve():
        rows_copy().wait_recv()
        tags_copy().wait_recv()
        got = nt_dot(pd[me], rows_in[...])
        voice_of = (lax.broadcasted_iota(jnp.int32, (panel, lanes), 0) // rank).astype(F32)
        back_out[...] = fold(jnp.where(voice_of + 1.0 == tags_in[0:1], got, 0.0))
        back_copy().start()

    def step(s, carry):
        xr[s, mx] = jnp.zeros((rank, rows), F32)
        for j in range(pieces):
            take(s, j)
            if j > 1:
                process(s, j - 1)
            if trade and j == early - 1:
                pl.when(is_host & (s == 2))(serve)
        process(s, PARTS)
        if trade:

            @pl.when(is_end & (s == 2))
            def _():
                back_copy().wait_recv()
                xr[s, mx] += jnp.dot(
                    back_in[...],
                    perm_v[...],
                    precision=lax.Precision.HIGHEST,
                    preferred_element_type=F32,
                )

        pl.when(busy(s))(lambda: send_rank(s))
        pl.when(busy(s - 1))(lambda: settle(s - 1))
        return carry

    if trade:
        keep = lanes - rows_out.shape[0]
        if keep:
            rows_in[rows_out.shape[0] :] = jnp.zeros((keep, feat), BF16)
    lax.fori_loop(2, n, step, 0)
    pl.when(busy(n - 1))(lambda: settle(n - 1))

    def base_wait(i, carry):
        for p in range(1, t):
            xb_copy(i, p, peer(p)).wait_recv()
        acc = total[:, b_cols(i)]
        for x in range(t):
            acc = acc + xb[x, :, b_cols(i)].astype(F32)
        out[:, b_cols(i)] = acc.astype(BF16)
        for p in range(1, t):
            xb_copy(i, p, mx).wait_send()
        return carry

    lax.fori_loop(0, tiles, base_wait, 0)

    own_sends(range(pieces), lambda c: c.wait_send())
    for p in range(1, t):
        xr_copy(0, p, mx).wait_send()
    if trade:

        @pl.when(is_end)
        def _():
            rows_copy().wait_send()
            tags_copy().wait_send()

        pl.when(is_host)(lambda: back_copy().wait_send())

    def drain(s, carry):
        def sent(o, direction):
            for j in range(pieces):

                def one():
                    pl.when(on_line(me + direction))(lambda: z_copy(direction, o, j).wait_send())
                    sib_copy(o, j, core).wait_send()

                if j == 0 or not trade:
                    one()
                else:
                    pl.when(jnp.logical_not(is_end & (s == 1)))(one)
            for p in range(1, t):
                xu_copy(o, p).wait_send()
                xu_arrival(o, p, core, sx_send, sx_recv).wait_send()

        both(s, sent)

        @pl.when(busy(s))
        def _():
            for p in range(1, t):
                xr_copy(s, p, mx).wait_send()

        return carry

    lax.fori_loop(1, n, drain, 0)


def local(n, t, activations, row_voice, slot_table, weight, down, up):
    rows, feat = activations.shape
    voices, rank, span = up.shape
    width = weight.shape[1]
    panel = voices * rank
    tiles = width // min(TILE, span)
    cap = max(2, rows // min(n, 8))
    sent_rows = -(-cap // 16) * 16
    lanes = -(-cap // 128) * 128
    any_spec = pl.BlockSpec(memory_space=pl.ANY)
    dma = pltpu.SemaphoreType.DMA
    return pl.pallas_call(
        functools.partial(kernel, n, t, voices, rank, cap),
        out_shape=jax.ShapeDtypeStruct((rows, width), BF16),
        in_specs=[
            pl.BlockSpec(memory_space=pltpu.VMEM),
            pl.BlockSpec(memory_space=pltpu.SMEM),
            any_spec,
            any_spec,
            any_spec,
            any_spec,
        ],
        out_specs=pl.BlockSpec(memory_space=pltpu.VMEM),
        scratch_shapes=[
            pltpu.VMEM((rows, feat), BF16),
            pltpu.VMEM((feat, width), BF16),
            pltpu.VMEM((n, panel, feat), BF16),
            pltpu.VMEM((t, n * panel, span), BF16),
            pltpu.VMEM((t, rows, width), BF16),
            pltpu.VMEM((rows, width), F32),
            pltpu.VMEM((n, t, rank, rows), F32),
            pltpu.VMEM((1, rows), jnp.int32),
            pltpu.VMEM((2, panel, rows), F32),
            pltpu.VMEM((lanes, rows), F32),
            pltpu.VMEM((sent_rows, feat), BF16),
            pltpu.VMEM((8, lanes), F32),
            pltpu.VMEM((lanes, feat), BF16),
            pltpu.VMEM((8, lanes), F32),
            pltpu.VMEM((rank, lanes), F32),
            pltpu.VMEM((rank, lanes), F32),
            dma((2, n, PARTS + 1)),
            dma((n, PARTS + 1)),
            dma((n, PARTS + 1)),
            dma((n, PARTS + 1)),
            dma((n, t)),
            dma((n, t)),
            dma((n, t)),
            dma((n, t)),
            dma((tiles, t)),
            dma((tiles, t)),
            dma((n, t)),
            dma((n, t)),
            dma((tiles,)),
            dma((3,)),
            dma((3,)),
            dma((3,)),
        ],
        compiler_params=pltpu.CompilerParams(
            collective_id=0, has_side_effects=True, vmem_limit_bytes=56 * 1024 * 1024
        ),
    )(
        row_voice.reshape(1, rows),
        slot_table,
        activations,
        weight,
        down.reshape(panel, feat),
        up.reshape(panel, span),
    )


def solution(mesh):
    in_specs = (
        P(("groups", "replica", "sub"), "tensor"),
        P(("groups", "replica", "sub")),
        P("groups"),
        P("tensor", None),
        P(("groups", "replica"), None, "tensor"),
        P(("groups", "replica"), None, "tensor"),
    )
    out_specs = P(("groups", "replica", "sub"), None)
    body = functools.partial(local, mesh.shape["replica"], mesh.shape["tensor"])
    return jax.shard_map(body, mesh=mesh, in_specs=in_specs, out_specs=out_specs, check_vma=False)
```

```python
import functools

import jax
import jax.numpy as jnp
from jax import lax
from jax.experimental import pallas as pl
from jax.experimental.pallas import tpu as pltpu
from jax.sharding import PartitionSpec as P

DELTA_GAIN = 2.0
MESH = pl.DeviceIdType.MESH
TILE = 256
PARTS = 4
F32 = jnp.float32
BF16 = jnp.bfloat16


def kernel(
    n,
    t,
    voices,
    rank,
    cap,
    voice,
    table,
    act,
    weight,
    down,
    up,
    out,
    act_v,
    w_v,
    pd,
    pu,
    xb,
    total,
    xr,
    slot_v,
    made_v,
    perm_v,
    rows_out,
    tags_out,
    rows_in,
    tags_in,
    back_out,
    back_in,
    z_send,
    z_recv,
    sib_send,
    sib_recv,
    xu_send,
    xu_recv,
    sx_send,
    sx_recv,
    xb_send,
    xb_recv,
    xr_send,
    xr_recv,
    w_sem,
    loc_sem,
    trade_send,
    trade_recv,
):
    rows, feat = act_v.shape
    width = w_v.shape[1]
    span = up.shape[1]
    panel = voices * rank
    tile = min(TILE, span)
    tiles = width // tile
    me = lax.axis_index("replica")
    mx = lax.axis_index("tensor")
    core = lax.axis_index("sub")
    hu, hd, qd = span // 2, feat // 2, feat // (2 * PARTS)
    pieces = PARTS + 1
    trade = n >= 4
    is_end = ((me == 0) | (me == n - 1)) if trade else (me < 0)
    is_host = ((me == 1) | (me == n - 2)) if trade else (me < 0)
    inward = jnp.where(me == 0, 1, -1)
    outward = jnp.where(me == 1, -1, 1)
    lanes = perm_v.shape[0]

    def peer(p):
        return lax.rem(mx + p, t)

    def slab(o):
        return pl.ds(pl.multiple_of(o * panel, 16), panel)

    def u_cols(k):
        return pl.ds(pl.multiple_of(k * hu, 128), hu)

    def d_cols(k, j):
        return pl.ds(pl.multiple_of(k * hd + (j - 1) * qd, 128), qd)

    def piece(o, j, k):
        if j == 0:
            return pu.at[mx, slab(o), u_cols(k)]
        return pd.at[o, :, d_cols(k, j)]

    def own_piece(j):
        if j == 0:
            return up.at[:, u_cols(core)]
        return down.at[:, d_cols(core, j)]

    def z_copy(direction, o, j, own=False):
        return pltpu.make_async_remote_copy(
            src_ref=own_piece(j) if own else piece(o, j, core),
            dst_ref=piece(o, j, core),
            send_sem=z_send.at[(direction + 1) // 2, o, j],
            recv_sem=z_recv.at[o, j],
            device_id={"replica": me + direction},
            device_id_type=MESH,
        )

    def sib_copy(o, j, k):
        return pltpu.make_async_remote_copy(
            src_ref=piece(o, j, k),
            dst_ref=piece(o, j, k),
            send_sem=sib_send.at[o, j],
            recv_sem=sib_recv.at[o, j],
            device_id={"sub": 1 - core},
            device_id_type=MESH,
        )

    def xu_copy(o, p):
        return pltpu.make_async_remote_copy(
            src_ref=piece(o, 0, core),
            dst_ref=piece(o, 0, core),
            send_sem=xu_send.at[o, p],
            recv_sem=xu_recv.at[o, t - p],
            device_id={"tensor": peer(p)},
            device_id_type=MESH,
        )

    def xu_arrival(o, p, k, send, recv):
        where = pu.at[peer(p), slab(o), u_cols(k)]
        return pltpu.make_async_remote_copy(
            src_ref=where,
            dst_ref=where,
            send_sem=send.at[o, p],
            recv_sem=recv.at[o, p],
            device_id={"sub": 1 - core},
            device_id_type=MESH,
        )

    def b_cols(i):
        return pl.ds(pl.multiple_of(i * tile, 128), tile)

    def xb_copy(i, p, owner):
        return pltpu.make_async_remote_copy(
            src_ref=xb.at[owner, :, b_cols(i)],
            dst_ref=xb.at[owner, :, b_cols(i)],
            send_sem=xb_send.at[i, p],
            recv_sem=xb_recv.at[i, t - p],
            device_id={"tensor": peer(p)},
            device_id_type=MESH,
        )

    def xr_copy(s, p, owner):
        return pltpu.make_async_remote_copy(
            src_ref=xr.at[s, owner],
            dst_ref=xr.at[s, owner],
            send_sem=xr_send.at[s, p],
            recv_sem=xr_recv.at[s, t - p],
            device_id={"tensor": peer(p)},
            device_id_type=MESH,
        )

    def trade_copy(k, src, dst, direction):
        return pltpu.make_async_remote_copy(
            src_ref=src,
            dst_ref=dst,
            send_sem=trade_send.at[k],
            recv_sem=trade_recv.at[k],
            device_id={"replica": me + direction},
            device_id_type=MESH,
        )

    def rows_copy():
        return trade_copy(0, rows_out, rows_in.at[pl.ds(0, rows_out.shape[0])], inward)

    def tags_copy():
        return trade_copy(1, tags_out, tags_in, inward)

    def back_copy():
        return trade_copy(2, back_out, back_in, outward)

    def w_copy(i):
        return pltpu.make_async_copy(weight.at[:, b_cols(i)], w_v.at[:, b_cols(i)], w_sem.at[i])

    barrier = pltpu.get_barrier_semaphore()

    def greet(device):
        pl.semaphore_signal(barrier, inc=1, device_id=device, device_id_type=MESH)

    act_copy = pltpu.make_async_copy(act, act_v, loc_sem.at[0])
    down_copy = pltpu.make_async_copy(down, pd.at[me], loc_sem.at[1])
    up_copy = pltpu.make_async_copy(up, pu.at[mx, slab(me)], loc_sem.at[2])
    greet({"sub": 1 - core})
    for p in range(1, t):
        greet({"tensor": peer(p)})
    pl.when(me > 0)(lambda: greet({"replica": me - 1}))
    pl.when(me < n - 1)(lambda: greet({"replica": me + 1}))
    act_copy.start()
    down_copy.start()
    up_copy.start()
    order = [lax.rem((mx + 1) * (span // tile) + i, tiles) for i in range(tiles)]
    for i in order:
        w_copy(i).start()
    ends = (me == 0).astype(jnp.int32) + (me == n - 1).astype(jnp.int32)
    pl.semaphore_wait(barrier, t + 2 - ends)

    def on_line(o):
        return (o >= 0) & (o < n)

    def own_send(direction, j, act_on):
        to = me + direction
        wanted = on_line(to)
        if trade and j > 0:
            wanted = wanted & (to > 0) & (to < n - 1)
        pl.when(wanted)(lambda: act_on(z_copy(direction, me, j, True)))

    def own_sends(js, act_on):
        for j in js:
            for direction in (-1, 1):
                own_send(direction, j, act_on)

    own_sends(range(pieces), lambda c: c.start())

    act_copy.wait()

    row_voice = voice[...].reshape(1, rows)

    def slot_step(v, slot):
        return jnp.where(row_voice == v, table[v], slot)

    slot_v[...] = lax.fori_loop(0, table.shape[0], slot_step, jnp.zeros_like(row_voice))
    section = lax.broadcasted_iota(jnp.int32, (panel, rows), 0) // rank

    def mask_of(o):
        return section == (slot_v[...] - o * voices)

    def fold(kept):
        return kept.reshape(voices, rank, kept.shape[1]).sum(axis=0)

    def nt_dot(a, b):
        return lax.dot_general(a, b, (((1,), (1,)), ((), ())), preferred_element_type=F32)

    def tn_dot(a, b):
        return lax.dot_general(a, b, (((0,), (0,)), ((), ())), preferred_element_type=F32)

    def send_rank(s):
        for p in range(1, t):
            xr_copy(s, p, mx).start()

    def rank_sum(s):
        for p in range(1, t):
            xr_copy(s, p, peer(p)).wait_recv()
        acc = xr[s, 0]
        for x in range(1, t):
            acc = acc + xr[s, x]
        return (DELTA_GAIN * acc.astype(BF16).astype(F32)).astype(BF16)

    def widen(o, narrowed):
        return jnp.where(mask_of(o), jnp.tile(narrowed, (voices, 1)), jnp.zeros((), BF16))

    def both(s, act_on):
        pl.when(me - s >= 0)(lambda: act_on(me - s, 1))
        pl.when(me + s < n)(lambda: act_on(me + s, -1))

    def take(s, j):
        def one(o, direction):
            z_copy(direction, o, j).wait_recv()
            pl.when(on_line(me + direction))(lambda: z_copy(direction, o, j).start())
            sib_copy(o, j, core).start()
            if j == 0:
                for p in range(1, t):
                    xu_copy(o, p).start()

        both(s, one)

    def process(s, j):
        def one(o, direction):
            side = (direction + 1) // 2
            sib_copy(o, j, 1 - core).wait_recv()
            got = nt_dot(pd[o, :, d_cols(0, j)], act_v[:, d_cols(0, j)])
            got = got + nt_dot(pd[o, :, d_cols(1, j)], act_v[:, d_cols(1, j)])
            if j > 1:
                got = got + made_v[side]
            if j < PARTS:
                made_v[side] = got
            else:
                xr[s, mx] += fold(jnp.where(mask_of(o), got, 0.0))

        both(s, one)

    def relay(o):
        for p in range(1, t):
            xu_arrival(o, p, core, xu_send, xu_recv).wait_recv()
            xu_arrival(o, p, core, sx_send, sx_recv).start()

    def settle_owner(o, narrowed):
        wide = widen(o, narrowed)
        sib_copy(o, 0, 1 - core).wait_recv()
        for p in range(1, t):
            xu_arrival(o, p, 1 - core, sx_send, sx_recv).wait_recv()
        for x in range(t):
            total[:, x * span : (x + 1) * span] += tn_dot(wide, pu[x, slab(o)])

    def settle(s):
        both(s, lambda o, direction: relay(o))
        if trade:
            pl.when(is_end & (s == 2))(lambda: relay(me + inward))
        narrowed = rank_sum(s)
        both(s, lambda o, direction: settle_owner(o, narrowed))
        if trade:
            pl.when(is_end & (s == 2))(lambda: settle_owner(me + inward, narrowed))

    def busy(s):
        some = on_line(me - s) | on_line(me + s)
        if trade:
            some = some & jnp.logical_not(is_end & (s == 1))
        return some

    down_copy.wait()
    xr[0, mx] = fold(jnp.where(mask_of(me), nt_dot(pd[me], act_v[...]), 0.0))
    send_rank(0)
    up_copy.wait()

    def base_tile(i, extra=None):
        w_copy(i).wait()
        part = jnp.dot(act_v[...], w_v[:, b_cols(i)], preferred_element_type=F32)
        if extra is not None:
            part = part + extra
        xb[mx, :, b_cols(i)] = part.astype(BF16)
        for p in range(1, t):
            xb_copy(i, p, mx).start()

    def early_take(j):
        if j == 0 or not trade:
            take(1, j)
        else:
            pl.when(jnp.logical_not(is_end))(lambda: take(1, j))

    others = tiles - span // tile
    for k in range(others):
        base_tile(order[k])
        early_take(k)

    if trade:

        @pl.when(is_end)
        def _():
            target = me + inward
            local_slot = slot_v[...] - target * voices
            chosen = (local_slot >= 0) & (local_slot < voices)
            ones = chosen.astype(F32)
            up_to = lax.broadcasted_iota(jnp.int32, (rows, rows), 0) <= lax.broadcasted_iota(
                jnp.int32, (rows, rows), 1
            )
            counted = jnp.dot(
                jnp.broadcast_to(ones, (8, rows)).astype(BF16),
                up_to.astype(F32).astype(BF16),
                preferred_element_type=F32,
            )[0:1]
            place = lax.broadcasted_iota(jnp.int32, (lanes, rows), 0).astype(F32) + 1.0
            perm = jnp.where((place == counted) & chosen, 1.0, 0.0)
            perm_v[...] = perm
            picked = perm.astype(BF16)
            rows_out[...] = jnp.dot(
                picked[: rows_out.shape[0]], act_v[...], preferred_element_type=F32
            ).astype(BF16)
            tag = jnp.where(chosen, local_slot + 1, 0).astype(F32)
            tags_out[...] = nt_dot(jnp.broadcast_to(tag, (8, rows)).astype(BF16), picked)
            tags_copy().start()
            rows_copy().start()

    wide0 = widen(me, rank_sum(0))
    per = span // tile
    for k in range(per):
        cols = pl.ds(k * tile, tile)
        base_tile(order[others + k], tn_dot(wide0, pu[mx, slab(me), cols]))
        if others + k < pieces:
            early_take(others + k)
    for j in range(tiles, pieces):
        early_take(j)
    total[...] = jnp.zeros_like(total)

    @pl.when(busy(1))
    def _():
        xr[1, mx] = jnp.zeros((rank, rows), F32)
        for j in range(1, pieces):
            process(1, j)
        send_rank(1)

    def serve():
        rows_copy().wait_recv()
        tags_copy().wait_recv()
        got = nt_dot(pd[me], rows_in[...])
        voice_of = (lax.broadcasted_iota(jnp.int32, (panel, lanes), 0) // rank).astype(F32)
        back_out[...] = fold(jnp.where(voice_of + 1.0 == tags_in[0:1], got, 0.0))
        back_copy().start()

    def step(s, carry):
        xr[s, mx] = jnp.zeros((rank, rows), F32)
        for j in range(pieces):
            take(s, j)
            if j > 1:
                process(s, j - 1)
            if trade and j == 2:
                pl.when(is_host & (s == 2))(serve)
        process(s, PARTS)
        if trade:

            @pl.when(is_end & (s == 2))
            def _():
                back_copy().wait_recv()
                xr[s, mx] += jnp.dot(
                    back_in[...],
                    perm_v[...],
                    precision=lax.Precision.HIGHEST,
                    preferred_element_type=F32,
                )

        pl.when(busy(s))(lambda: send_rank(s))
        pl.when(busy(s - 1))(lambda: settle(s - 1))
        return carry

    if trade:
        keep = lanes - rows_out.shape[0]
        if keep:
            rows_in[rows_out.shape[0] :] = jnp.zeros((keep, feat), BF16)
    lax.fori_loop(2, n, step, 0)
    pl.when(busy(n - 1))(lambda: settle(n - 1))

    def base_wait(i, carry):
        for p in range(1, t):
            xb_copy(i, p, peer(p)).wait_recv()
        acc = total[:, b_cols(i)]
        for x in range(t):
            acc = acc + xb[x, :, b_cols(i)].astype(F32)
        out[:, b_cols(i)] = acc.astype(BF16)
        for p in range(1, t):
            xb_copy(i, p, mx).wait_send()
        return carry

    lax.fori_loop(0, tiles, base_wait, 0)

    own_sends(range(pieces), lambda c: c.wait_send())
    for p in range(1, t):
        xr_copy(0, p, mx).wait_send()
    if trade:

        @pl.when(is_end)
        def _():
            rows_copy().wait_send()
            tags_copy().wait_send()

        pl.when(is_host)(lambda: back_copy().wait_send())

    def drain(s, carry):
        def sent(o, direction):
            for j in range(pieces):

                def one():
                    pl.when(on_line(me + direction))(lambda: z_copy(direction, o, j).wait_send())
                    sib_copy(o, j, core).wait_send()

                if j == 0 or not trade:
                    one()
                else:
                    pl.when(jnp.logical_not(is_end & (s == 1)))(one)
            for p in range(1, t):
                xu_copy(o, p).wait_send()
                xu_arrival(o, p, core, sx_send, sx_recv).wait_send()

        both(s, sent)

        @pl.when(busy(s))
        def _():
            for p in range(1, t):
                xr_copy(s, p, mx).wait_send()

        return carry

    lax.fori_loop(1, n, drain, 0)


def local(n, t, activations, row_voice, slot_table, weight, down, up):
    rows, feat = activations.shape
    voices, rank, span = up.shape
    width = weight.shape[1]
    panel = voices * rank
    tiles = width // min(TILE, span)
    cap = max(2, rows // min(n, 8))
    sent_rows = -(-cap // 16) * 16
    lanes = -(-cap // 128) * 128
    any_spec = pl.BlockSpec(memory_space=pl.ANY)
    dma = pltpu.SemaphoreType.DMA
    return pl.pallas_call(
        functools.partial(kernel, n, t, voices, rank, cap),
        out_shape=jax.ShapeDtypeStruct((rows, width), BF16),
        in_specs=[
            pl.BlockSpec(memory_space=pltpu.VMEM),
            pl.BlockSpec(memory_space=pltpu.SMEM),
            any_spec,
            any_spec,
            any_spec,
            any_spec,
        ],
        out_specs=pl.BlockSpec(memory_space=pltpu.VMEM),
        scratch_shapes=[
            pltpu.VMEM((rows, feat), BF16),
            pltpu.VMEM((feat, width), BF16),
            pltpu.VMEM((n, panel, feat), BF16),
            pltpu.VMEM((t, n * panel, span), BF16),
            pltpu.VMEM((t, rows, width), BF16),
            pltpu.VMEM((rows, width), F32),
            pltpu.VMEM((n, t, rank, rows), F32),
            pltpu.VMEM((1, rows), jnp.int32),
            pltpu.VMEM((2, panel, rows), F32),
            pltpu.VMEM((lanes, rows), F32),
            pltpu.VMEM((sent_rows, feat), BF16),
            pltpu.VMEM((8, lanes), F32),
            pltpu.VMEM((lanes, feat), BF16),
            pltpu.VMEM((8, lanes), F32),
            pltpu.VMEM((rank, lanes), F32),
            pltpu.VMEM((rank, lanes), F32),
            dma((2, n, PARTS + 1)),
            dma((n, PARTS + 1)),
            dma((n, PARTS + 1)),
            dma((n, PARTS + 1)),
            dma((n, t)),
            dma((n, t)),
            dma((n, t)),
            dma((n, t)),
            dma((tiles, t)),
            dma((tiles, t)),
            dma((n, t)),
            dma((n, t)),
            dma((tiles,)),
            dma((3,)),
            dma((3,)),
            dma((3,)),
        ],
        compiler_params=pltpu.CompilerParams(
            collective_id=0, has_side_effects=True, vmem_limit_bytes=56 * 1024 * 1024
        ),
    )(
        row_voice,
        slot_table,
        activations,
        weight,
        down.reshape(panel, feat),
        up.reshape(panel, span),
    )


def solution(mesh):
    in_specs = (
        P(("groups", "replica", "sub"), "tensor"),
        P(("groups", "replica", "sub")),
        P("groups"),
        P("tensor", None),
        P(("groups", "replica"), None, "tensor"),
        P(("groups", "replica"), None, "tensor"),
    )
    out_specs = P(("groups", "replica", "sub"), None)
    body = functools.partial(local, mesh.shape["replica"], mesh.shape["tensor"])
    return jax.shard_map(body, mesh=mesh, in_specs=in_specs, out_specs=out_specs, check_vma=False)
```

```python
import functools

import jax
import jax.numpy as jnp
from jax import lax
from jax.experimental import pallas as pl
from jax.experimental.pallas import tpu as pltpu
from jax.sharding import PartitionSpec as P

DELTA_GAIN = 2.0
MESH = pl.DeviceIdType.MESH
TILE = 256
PARTS = 4
F32 = jnp.float32
BF16 = jnp.bfloat16


def kernel(
    n,
    t,
    voices,
    rank,
    cap,
    voice,
    table,
    act,
    weight,
    down,
    up,
    out,
    act_v,
    w_v,
    pd,
    pu,
    xb,
    total,
    xr,
    slot_v,
    made_v,
    perm_v,
    rows_out,
    tags_out,
    rows_in,
    tags_in,
    back_out,
    back_in,
    z_send,
    z_recv,
    sib_send,
    sib_recv,
    xu_send,
    xu_recv,
    sx_send,
    sx_recv,
    xb_send,
    xb_recv,
    xr_send,
    xr_recv,
    w_sem,
    loc_sem,
    trade_send,
    trade_recv,
):
    rows, feat = act_v.shape
    width = w_v.shape[1]
    span = up.shape[1]
    panel = voices * rank
    tile = min(TILE, span)
    tiles = width // tile
    me = lax.axis_index("replica")
    mx = lax.axis_index("tensor")
    core = lax.axis_index("sub")
    hu, hd, qd = span // 2, feat // 2, feat // (2 * PARTS)
    pieces = PARTS + 1
    trade = n >= 4
    is_end = ((me == 0) | (me == n - 1)) if trade else (me < 0)
    is_host = ((me == 1) | (me == n - 2)) if trade else (me < 0)
    inward = jnp.where(me == 0, 1, -1)
    outward = jnp.where(me == 1, -1, 1)
    lanes = perm_v.shape[0]

    def peer(p):
        return lax.rem(mx + p, t)

    def slab(o):
        return pl.ds(pl.multiple_of(o * panel, 16), panel)

    def u_cols(k):
        return pl.ds(pl.multiple_of(k * hu, 128), hu)

    def d_cols(k, j):
        return pl.ds(pl.multiple_of(k * hd + (j - 1) * qd, 128), qd)

    def piece(o, j, k):
        if j == 0:
            return pu.at[mx, slab(o), u_cols(k)]
        return pd.at[o, :, d_cols(k, j)]

    def own_piece(j):
        if j == 0:
            return up.at[:, u_cols(core)]
        return down.at[:, d_cols(core, j)]

    def z_copy(direction, o, j, own=False):
        return pltpu.make_async_remote_copy(
            src_ref=own_piece(j) if own else piece(o, j, core),
            dst_ref=piece(o, j, core),
            send_sem=z_send.at[(direction + 1) // 2, o, j],
            recv_sem=z_recv.at[o, j],
            device_id={"replica": me + direction},
            device_id_type=MESH,
        )

    def sib_copy(o, j, k):
        return pltpu.make_async_remote_copy(
            src_ref=piece(o, j, k),
            dst_ref=piece(o, j, k),
            send_sem=sib_send.at[o, j],
            recv_sem=sib_recv.at[o, j],
            device_id={"sub": 1 - core},
            device_id_type=MESH,
        )

    def xu_copy(o, p):
        return pltpu.make_async_remote_copy(
            src_ref=piece(o, 0, core),
            dst_ref=piece(o, 0, core),
            send_sem=xu_send.at[o, p],
            recv_sem=xu_recv.at[o, t - p],
            device_id={"tensor": peer(p)},
            device_id_type=MESH,
        )

    def xu_arrival(o, p, k, send, recv):
        where = pu.at[peer(p), slab(o), u_cols(k)]
        return pltpu.make_async_remote_copy(
            src_ref=where,
            dst_ref=where,
            send_sem=send.at[o, p],
            recv_sem=recv.at[o, p],
            device_id={"sub": 1 - core},
            device_id_type=MESH,
        )

    def b_cols(i):
        return pl.ds(pl.multiple_of(i * tile, 128), tile)

    def xb_copy(i, p, owner):
        return pltpu.make_async_remote_copy(
            src_ref=xb.at[owner, :, b_cols(i)],
            dst_ref=xb.at[owner, :, b_cols(i)],
            send_sem=xb_send.at[i, p],
            recv_sem=xb_recv.at[i, t - p],
            device_id={"tensor": peer(p)},
            device_id_type=MESH,
        )

    def xr_copy(s, p, owner):
        return pltpu.make_async_remote_copy(
            src_ref=xr.at[s, owner],
            dst_ref=xr.at[s, owner],
            send_sem=xr_send.at[s, p],
            recv_sem=xr_recv.at[s, t - p],
            device_id={"tensor": peer(p)},
            device_id_type=MESH,
        )

    def trade_copy(k, src, dst, direction):
        return pltpu.make_async_remote_copy(
            src_ref=src,
            dst_ref=dst,
            send_sem=trade_send.at[k],
            recv_sem=trade_recv.at[k],
            device_id={"replica": me + direction},
            device_id_type=MESH,
        )

    def rows_copy():
        return trade_copy(0, rows_out, rows_in.at[pl.ds(0, rows_out.shape[0])], inward)

    def tags_copy():
        return trade_copy(1, tags_out, tags_in, inward)

    def back_copy():
        return trade_copy(2, back_out, back_in, outward)

    def w_copy(i):
        return pltpu.make_async_copy(weight.at[:, b_cols(i)], w_v.at[:, b_cols(i)], w_sem.at[i])

    barrier = pltpu.get_barrier_semaphore()

    def greet(device):
        pl.semaphore_signal(barrier, inc=1, device_id=device, device_id_type=MESH)

    act_copy = pltpu.make_async_copy(act, act_v, loc_sem.at[0])
    down_copy = pltpu.make_async_copy(down, pd.at[me], loc_sem.at[1])
    up_copy = pltpu.make_async_copy(up, pu.at[mx, slab(me)], loc_sem.at[2])
    greet({"sub": 1 - core})
    for p in range(1, t):
        greet({"tensor": peer(p)})
    pl.when(me > 0)(lambda: greet({"replica": me - 1}))
    pl.when(me < n - 1)(lambda: greet({"replica": me + 1}))
    act_copy.start()
    down_copy.start()
    up_copy.start()
    order = [lax.rem((mx + 1) * (span // tile) + i, tiles) for i in range(tiles)]
    for i in order:
        w_copy(i).start()
    ends = (me == 0).astype(jnp.int32) + (me == n - 1).astype(jnp.int32)
    pl.semaphore_wait(barrier, t + 2 - ends)

    def on_line(o):
        return (o >= 0) & (o < n)

    def own_send(direction, j, act_on):
        to = me + direction
        wanted = on_line(to)
        if trade and j > 0:
            wanted = wanted & (to > 0) & (to < n - 1)
        pl.when(wanted)(lambda: act_on(z_copy(direction, me, j, True)))

    def own_sends(js, act_on):
        for j in js:
            for direction in (-1, 1):
                own_send(direction, j, act_on)

    own_sends(range(pieces), lambda c: c.start())

    act_copy.wait()

    row_voice = voice[...].reshape(1, rows)

    def slot_step(v, slot):
        return jnp.where(row_voice == v, table[v], slot)

    slot_v[...] = lax.fori_loop(0, table.shape[0], slot_step, jnp.zeros_like(row_voice))
    section = lax.broadcasted_iota(jnp.int32, (panel, rows), 0) // rank

    def mask_of(o):
        return section == (slot_v[...] - o * voices)

    def fold(kept):
        return kept.reshape(voices, rank, kept.shape[1]).sum(axis=0)

    def nt_dot(a, b):
        return lax.dot_general(a, b, (((1,), (1,)), ((), ())), preferred_element_type=F32)

    def tn_dot(a, b):
        return lax.dot_general(a, b, (((0,), (0,)), ((), ())), preferred_element_type=F32)

    def send_rank(s):
        for p in range(1, t):
            xr_copy(s, p, mx).start()

    def rank_sum(s):
        for p in range(1, t):
            xr_copy(s, p, peer(p)).wait_recv()
        acc = xr[s, 0]
        for x in range(1, t):
            acc = acc + xr[s, x]
        return (DELTA_GAIN * acc.astype(BF16).astype(F32)).astype(BF16)

    def widen(o, narrowed):
        return jnp.where(mask_of(o), jnp.tile(narrowed, (voices, 1)), jnp.zeros((), BF16))

    def both(s, act_on):
        pl.when(me - s >= 0)(lambda: act_on(me - s, 1))
        pl.when(me + s < n)(lambda: act_on(me + s, -1))

    def take(s, j):
        def one(o, direction):
            z_copy(direction, o, j).wait_recv()
            pl.when(on_line(me + direction))(lambda: z_copy(direction, o, j).start())
            sib_copy(o, j, core).start()
            if j == 0:
                for p in range(1, t):
                    xu_copy(o, p).start()

        both(s, one)

    def process(s, j):
        def one(o, direction):
            side = (direction + 1) // 2
            sib_copy(o, j, 1 - core).wait_recv()
            got = nt_dot(pd[o, :, d_cols(0, j)], act_v[:, d_cols(0, j)])
            got = got + nt_dot(pd[o, :, d_cols(1, j)], act_v[:, d_cols(1, j)])
            if j > 1:
                got = got + made_v[side]
            if j < PARTS:
                made_v[side] = got
            else:
                xr[s, mx] += fold(jnp.where(mask_of(o), got, 0.0))

        both(s, one)

    def relay(o):
        for p in range(1, t):
            xu_arrival(o, p, core, xu_send, xu_recv).wait_recv()
            xu_arrival(o, p, core, sx_send, sx_recv).start()

    def settle_owner(o, narrowed):
        wide = widen(o, narrowed)
        sib_copy(o, 0, 1 - core).wait_recv()
        for p in range(1, t):
            xu_arrival(o, p, 1 - core, sx_send, sx_recv).wait_recv()
        for x in range(t):
            total[:, x * span : (x + 1) * span] += tn_dot(wide, pu[x, slab(o)])

    def settle(s):
        both(s, lambda o, direction: relay(o))
        if trade:
            pl.when(is_end & (s == 2))(lambda: relay(me + inward))
        narrowed = rank_sum(s)
        both(s, lambda o, direction: settle_owner(o, narrowed))
        if trade:
            pl.when(is_end & (s == 2))(lambda: settle_owner(me + inward, narrowed))

    def busy(s):
        some = on_line(me - s) | on_line(me + s)
        if trade:
            some = some & jnp.logical_not(is_end & (s == 1))
        return some

    down_copy.wait()
    xr[0, mx] = fold(jnp.where(mask_of(me), nt_dot(pd[me], act_v[...]), 0.0))
    send_rank(0)
    up_copy.wait()

    def base_tile(i, extra=None):
        w_copy(i).wait()
        part = jnp.dot(act_v[...], w_v[:, b_cols(i)], preferred_element_type=F32)
        if extra is not None:
            part = part + extra
        xb[mx, :, b_cols(i)] = part.astype(BF16)
        for p in range(1, t):
            xb_copy(i, p, mx).start()

    def early_take(j):
        if j == 0 or not trade:
            take(1, j)
        else:
            pl.when(jnp.logical_not(is_end))(lambda: take(1, j))

    others = tiles - span // tile
    for k in range(others):
        base_tile(order[k])
        early_take(k)

    if trade:

        @pl.when(is_end)
        def _():
            target = me + inward
            local_slot = slot_v[...] - target * voices
            chosen = (local_slot >= 0) & (local_slot < voices)
            ones = chosen.astype(F32)
            up_to = lax.broadcasted_iota(jnp.int32, (rows, rows), 0) <= lax.broadcasted_iota(
                jnp.int32, (rows, rows), 1
            )
            counted = jnp.dot(
                jnp.broadcast_to(ones, (8, rows)).astype(BF16),
                up_to.astype(F32).astype(BF16),
                preferred_element_type=F32,
            )[0:1]
            place = lax.broadcasted_iota(jnp.int32, (lanes, rows), 0).astype(F32) + 1.0
            perm = jnp.where((place == counted) & chosen, 1.0, 0.0)
            perm_v[...] = perm
            picked = perm.astype(BF16)
            rows_out[...] = jnp.dot(
                picked[: rows_out.shape[0]], act_v[...], preferred_element_type=F32
            ).astype(BF16)
            tag = jnp.where(chosen, local_slot + 1, 0).astype(F32)
            tags_out[...] = nt_dot(jnp.broadcast_to(tag, (8, rows)).astype(BF16), picked)
            tags_copy().start()
            rows_copy().start()

    wide0 = widen(me, rank_sum(0))
    per = span // tile
    for k in range(per):
        cols = pl.ds(k * tile, tile)
        base_tile(order[others + k], tn_dot(wide0, pu[mx, slab(me), cols]))
        if others + k < pieces:
            early_take(others + k)
    for j in range(tiles, pieces):
        early_take(j)
    total[...] = jnp.zeros_like(total)

    @pl.when(busy(1))
    def _():
        xr[1, mx] = jnp.zeros((rank, rows), F32)
        for j in range(1, pieces):
            process(1, j)
        send_rank(1)

    def serve():
        rows_copy().wait_recv()
        tags_copy().wait_recv()
        got = nt_dot(pd[me], rows_in[...])
        voice_of = (lax.broadcasted_iota(jnp.int32, (panel, lanes), 0) // rank).astype(F32)
        back_out[...] = fold(jnp.where(voice_of + 1.0 == tags_in[0:1], got, 0.0))
        back_copy().start()

    def step(s, carry):
        xr[s, mx] = jnp.zeros((rank, rows), F32)
        for j in range(pieces):
            take(s, j)
            if j > 1:
                process(s, j - 1)
            if trade and j == 2:
                pl.when(is_host & (s == 2))(serve)
        process(s, PARTS)
        if trade:

            @pl.when(is_end & (s == 2))
            def _():
                back_copy().wait_recv()
                xr[s, mx] += jnp.dot(
                    back_in[...],
                    perm_v[...],
                    precision=lax.Precision.HIGHEST,
                    preferred_element_type=F32,
                )

        pl.when(busy(s))(lambda: send_rank(s))
        pl.when(busy(s - 1))(lambda: settle(s - 1))
        return carry

    if trade:
        keep = lanes - rows_out.shape[0]
        if keep:
            rows_in[rows_out.shape[0] :] = jnp.zeros((keep, feat), BF16)
    lax.fori_loop(2, n, step, 0)
    pl.when(busy(n - 1))(lambda: settle(n - 1))

    def base_wait(i, carry):
        for p in range(1, t):
            xb_copy(i, p, peer(p)).wait_recv()
        acc = total[:, b_cols(i)]
        for x in range(t):
            acc = acc + xb[x, :, b_cols(i)].astype(F32)
        out[:, b_cols(i)] = acc.astype(BF16)
        for p in range(1, t):
            xb_copy(i, p, mx).wait_send()
        return carry

    lax.fori_loop(0, tiles, base_wait, 0)

    own_sends(range(pieces), lambda c: c.wait_send())
    for p in range(1, t):
        xr_copy(0, p, mx).wait_send()
    if trade:

        @pl.when(is_end)
        def _():
            rows_copy().wait_send()
            tags_copy().wait_send()

        pl.when(is_host)(lambda: back_copy().wait_send())

    def drain(s, carry):
        def sent(o, direction):
            for j in range(pieces):

                def one():
                    pl.when(on_line(me + direction))(lambda: z_copy(direction, o, j).wait_send())
                    sib_copy(o, j, core).wait_send()

                if j == 0 or not trade:
                    one()
                else:
                    pl.when(jnp.logical_not(is_end & (s == 1)))(one)
            for p in range(1, t):
                xu_copy(o, p).wait_send()
                xu_arrival(o, p, core, sx_send, sx_recv).wait_send()

        both(s, sent)

        @pl.when(busy(s))
        def _():
            for p in range(1, t):
                xr_copy(s, p, mx).wait_send()

        return carry

    lax.fori_loop(1, n, drain, 0)


def local(n, t, activations, row_voice, slot_table, weight, down, up):
    rows, feat = activations.shape
    voices, rank, span = up.shape
    width = weight.shape[1]
    panel = voices * rank
    tiles = width // min(TILE, span)
    cap = max(2, rows // min(n, 8))
    sent_rows = -(-cap // 16) * 16
    lanes = -(-cap // 128) * 128
    any_spec = pl.BlockSpec(memory_space=pl.ANY)
    dma = pltpu.SemaphoreType.DMA
    return pl.pallas_call(
        functools.partial(kernel, n, t, voices, rank, cap),
        out_shape=pltpu.VMEM((rows, width), BF16),
        in_specs=[
            pl.BlockSpec(memory_space=pltpu.VMEM),
            pl.BlockSpec(memory_space=pltpu.SMEM),
            any_spec,
            any_spec,
            any_spec,
            any_spec,
        ],
        out_specs=pl.BlockSpec(memory_space=pltpu.VMEM),
        scratch_shapes=[
            pltpu.VMEM((rows, feat), BF16),
            pltpu.VMEM((feat, width), BF16),
            pltpu.VMEM((n, panel, feat), BF16),
            pltpu.VMEM((t, n * panel, span), BF16),
            pltpu.VMEM((t, rows, width), BF16),
            pltpu.VMEM((rows, width), F32),
            pltpu.VMEM((n, t, rank, rows), F32),
            pltpu.VMEM((1, rows), jnp.int32),
            pltpu.VMEM((2, panel, rows), F32),
            pltpu.VMEM((lanes, rows), F32),
            pltpu.VMEM((sent_rows, feat), BF16),
            pltpu.VMEM((8, lanes), F32),
            pltpu.VMEM((lanes, feat), BF16),
            pltpu.VMEM((8, lanes), F32),
            pltpu.VMEM((rank, lanes), F32),
            pltpu.VMEM((rank, lanes), F32),
            dma((2, n, PARTS + 1)),
            dma((n, PARTS + 1)),
            dma((n, PARTS + 1)),
            dma((n, PARTS + 1)),
            dma((n, t)),
            dma((n, t)),
            dma((n, t)),
            dma((n, t)),
            dma((tiles, t)),
            dma((tiles, t)),
            dma((n, t)),
            dma((n, t)),
            dma((tiles,)),
            dma((3,)),
            dma((3,)),
            dma((3,)),
        ],
        compiler_params=pltpu.CompilerParams(
            collective_id=0, has_side_effects=True, vmem_limit_bytes=56 * 1024 * 1024
        ),
    )(
        row_voice,
        slot_table,
        activations,
        weight,
        down.reshape(panel, feat),
        up.reshape(panel, span),
    )


def solution(mesh):
    in_specs = (
        P(("groups", "replica", "sub"), "tensor"),
        P(("groups", "replica", "sub")),
        P("groups"),
        P("tensor", None),
        P(("groups", "replica"), None, "tensor"),
        P(("groups", "replica"), None, "tensor"),
    )
    out_specs = P(("groups", "replica", "sub"), None)
    body = functools.partial(local, mesh.shape["replica"], mesh.shape["tensor"])
    return jax.shard_map(body, mesh=mesh, in_specs=in_specs, out_specs=out_specs, check_vma=False)
```

```python
import functools

import jax
import jax.numpy as jnp
from jax import lax
from jax.experimental import pallas as pl
from jax.experimental.pallas import tpu as pltpu
from jax.sharding import PartitionSpec as P

DELTA_GAIN = 2.0
MESH = pl.DeviceIdType.MESH
TILE = 256
PARTS = 4
F32 = jnp.float32
BF16 = jnp.bfloat16


def kernel(
    n,
    t,
    voices,
    rank,
    cap,
    voice,
    table,
    act,
    weight,
    down,
    up,
    out,
    act_v,
    w_v,
    pd,
    pu,
    xb,
    total,
    xr,
    slot_v,
    made_v,
    perm_v,
    rows_out,
    tags_out,
    rows_in,
    tags_in,
    back_out,
    back_in,
    z_send,
    z_recv,
    sib_send,
    sib_recv,
    xu_send,
    xu_recv,
    sx_send,
    sx_recv,
    xb_send,
    xb_recv,
    xr_send,
    xr_recv,
    w_sem,
    loc_sem,
    trade_send,
    trade_recv,
):
    rows, feat = act_v.shape
    width = w_v.shape[1]
    span = up.shape[1]
    panel = voices * rank
    tile = min(TILE, span)
    tiles = width // tile
    me = lax.axis_index("replica")
    mx = lax.axis_index("tensor")
    core = lax.axis_index("sub")
    hu, hd, qd = span // 2, feat // 2, feat // (2 * PARTS)
    pieces = PARTS + 1
    trade = n >= 4
    is_end = ((me == 0) | (me == n - 1)) if trade else (me < 0)
    is_host = ((me == 1) | (me == n - 2)) if trade else (me < 0)
    inward = jnp.where(me == 0, 1, -1)
    outward = jnp.where(me == 1, -1, 1)
    lanes = perm_v.shape[0]

    def peer(p):
        return lax.rem(mx + p, t)

    def slab(o):
        return pl.ds(pl.multiple_of(o * panel, 16), panel)

    def u_cols(k):
        return pl.ds(pl.multiple_of(k * hu, 128), hu)

    def d_cols(k, j):
        return pl.ds(pl.multiple_of(k * hd + (j - 1) * qd, 128), qd)

    def piece(o, j, k):
        if j == 0:
            return pu.at[mx, slab(o), u_cols(k)]
        return pd.at[o, :, d_cols(k, j)]

    def own_piece(j):
        if j == 0:
            return up.at[:, u_cols(core)]
        return down.at[:, d_cols(core, j)]

    def z_copy(direction, o, j, own=False):
        return pltpu.make_async_remote_copy(
            src_ref=own_piece(j) if own else piece(o, j, core),
            dst_ref=piece(o, j, core),
            send_sem=z_send.at[(direction + 1) // 2, o, j],
            recv_sem=z_recv.at[o, j],
            device_id={"replica": me + direction},
            device_id_type=MESH,
        )

    def sib_copy(o, j, k):
        return pltpu.make_async_remote_copy(
            src_ref=piece(o, j, k),
            dst_ref=piece(o, j, k),
            send_sem=sib_send.at[o, j],
            recv_sem=sib_recv.at[o, j],
            device_id={"sub": 1 - core},
            device_id_type=MESH,
        )

    def xu_copy(o, p):
        return pltpu.make_async_remote_copy(
            src_ref=piece(o, 0, core),
            dst_ref=piece(o, 0, core),
            send_sem=xu_send.at[o, p],
            recv_sem=xu_recv.at[o, t - p],
            device_id={"tensor": peer(p)},
            device_id_type=MESH,
        )

    def xu_arrival(o, p, k, send, recv):
        where = pu.at[peer(p), slab(o), u_cols(k)]
        return pltpu.make_async_remote_copy(
            src_ref=where,
            dst_ref=where,
            send_sem=send.at[o, p],
            recv_sem=recv.at[o, p],
            device_id={"sub": 1 - core},
            device_id_type=MESH,
        )

    def b_cols(i):
        return pl.ds(pl.multiple_of(i * tile, 128), tile)

    def xb_copy(i, p, owner):
        return pltpu.make_async_remote_copy(
            src_ref=xb.at[owner, :, b_cols(i)],
            dst_ref=xb.at[owner, :, b_cols(i)],
            send_sem=xb_send.at[i, p],
            recv_sem=xb_recv.at[i, t - p],
            device_id={"tensor": peer(p)},
            device_id_type=MESH,
        )

    def xr_copy(s, p, owner):
        return pltpu.make_async_remote_copy(
            src_ref=xr.at[s, owner],
            dst_ref=xr.at[s, owner],
            send_sem=xr_send.at[s, p],
            recv_sem=xr_recv.at[s, t - p],
            device_id={"tensor": peer(p)},
            device_id_type=MESH,
        )

    def trade_copy(k, src, dst, direction):
        return pltpu.make_async_remote_copy(
            src_ref=src,
            dst_ref=dst,
            send_sem=trade_send.at[k],
            recv_sem=trade_recv.at[k],
            device_id={"replica": me + direction},
            device_id_type=MESH,
        )

    def rows_copy():
        return trade_copy(0, rows_out, rows_in.at[pl.ds(0, rows_out.shape[0])], inward)

    def tags_copy():
        return trade_copy(1, tags_out, tags_in, inward)

    def back_copy():
        return trade_copy(2, back_out, back_in, outward)

    def w_copy(i):
        return pltpu.make_async_copy(weight.at[:, b_cols(i)], w_v.at[:, b_cols(i)], w_sem.at[i])

    barrier = pltpu.get_barrier_semaphore()

    def greet(device):
        pl.semaphore_signal(barrier, inc=1, device_id=device, device_id_type=MESH)

    act_copy = pltpu.make_async_copy(act, act_v, loc_sem.at[0])
    down_copy = pltpu.make_async_copy(down, pd.at[me], loc_sem.at[1])
    up_copy = pltpu.make_async_copy(up, pu.at[mx, slab(me)], loc_sem.at[2])
    greet({"sub": 1 - core})
    for p in range(1, t):
        greet({"tensor": peer(p)})
    pl.when(me > 0)(lambda: greet({"replica": me - 1}))
    pl.when(me < n - 1)(lambda: greet({"replica": me + 1}))
    act_copy.start()
    down_copy.start()
    up_copy.start()
    order = [lax.rem((mx + 1) * (span // tile) + i, tiles) for i in range(tiles)]
    for i in order:
        w_copy(i).start()
    ends = (me == 0).astype(jnp.int32) + (me == n - 1).astype(jnp.int32)
    pl.semaphore_wait(barrier, t + 2 - ends)

    def on_line(o):
        return (o >= 0) & (o < n)

    def own_send(direction, j, act_on):
        to = me + direction
        wanted = on_line(to)
        if trade and j > 0:
            wanted = wanted & (to > 0) & (to < n - 1)
        pl.when(wanted)(lambda: act_on(z_copy(direction, me, j, True)))

    def own_sends(js, act_on):
        for j in js:
            for direction in (-1, 1):
                own_send(direction, j, act_on)

    own_sends(range(pieces), lambda c: c.start())

    act_copy.wait()

    row_voice = voice[...].reshape(1, rows)

    def slot_step(v, slot):
        return jnp.where(row_voice == v, table[v], slot)

    slot_v[...] = lax.fori_loop(0, table.shape[0], slot_step, jnp.zeros_like(row_voice))
    section = lax.broadcasted_iota(jnp.int32, (panel, rows), 0) // rank

    def mask_of(o):
        return section == (slot_v[...] - o * voices)

    def fold(kept):
        return kept.reshape(voices, rank, kept.shape[1]).sum(axis=0)

    def nt_dot(a, b):
        return lax.dot_general(a, b, (((1,), (1,)), ((), ())), preferred_element_type=F32)

    def tn_dot(a, b):
        return lax.dot_general(a, b, (((0,), (0,)), ((), ())), preferred_element_type=F32)

    def send_rank(s):
        for p in range(1, t):
            xr_copy(s, p, mx).start()

    def rank_sum(s):
        for p in range(1, t):
            xr_copy(s, p, peer(p)).wait_recv()
        acc = xr[s, 0]
        for x in range(1, t):
            acc = acc + xr[s, x]
        return (DELTA_GAIN * acc.astype(BF16).astype(F32)).astype(BF16)

    def widen(o, narrowed):
        return jnp.where(mask_of(o), jnp.tile(narrowed, (voices, 1)), jnp.zeros((), BF16))

    def both(s, act_on):
        pl.when(me - s >= 0)(lambda: act_on(me - s, 1))
        pl.when(me + s < n)(lambda: act_on(me + s, -1))

    def take(s, j):
        def one(o, direction):
            z_copy(direction, o, j).wait_recv()
            pl.when(on_line(me + direction))(lambda: z_copy(direction, o, j).start())
            sib_copy(o, j, core).start()
            if j == 0:
                for p in range(1, t):
                    xu_copy(o, p).start()

        both(s, one)

    def process(s, j):
        def one(o, direction):
            side = (direction + 1) // 2
            sib_copy(o, j, 1 - core).wait_recv()
            got = nt_dot(pd[o, :, d_cols(0, j)], act_v[:, d_cols(0, j)])
            got = got + nt_dot(pd[o, :, d_cols(1, j)], act_v[:, d_cols(1, j)])
            if j > 1:
                got = got + made_v[side]
            if j < PARTS:
                made_v[side] = got
            else:
                xr[s, mx] += fold(jnp.where(mask_of(o), got, 0.0))

        both(s, one)

    def relay(o):
        for p in range(1, t):
            xu_arrival(o, p, core, xu_send, xu_recv).wait_recv()
            xu_arrival(o, p, core, sx_send, sx_recv).start()

    def settle_owner(o, narrowed):
        wide = widen(o, narrowed)
        sib_copy(o, 0, 1 - core).wait_recv()
        for p in range(1, t):
            xu_arrival(o, p, 1 - core, sx_send, sx_recv).wait_recv()
        for x in range(t):
            total[:, x * span : (x + 1) * span] += tn_dot(wide, pu[x, slab(o)])

    def settle(s):
        both(s, lambda o, direction: relay(o))
        if trade:
            pl.when(is_end & (s == 2))(lambda: relay(me + inward))
        narrowed = rank_sum(s)
        both(s, lambda o, direction: settle_owner(o, narrowed))
        if trade:
            pl.when(is_end & (s == 2))(lambda: settle_owner(me + inward, narrowed))

    def busy(s):
        some = on_line(me - s) | on_line(me + s)
        if trade:
            some = some & jnp.logical_not(is_end & (s == 1))
        return some

    down_copy.wait()
    xr[0, mx] = fold(jnp.where(mask_of(me), nt_dot(pd[me], act_v[...]), 0.0))
    send_rank(0)
    up_copy.wait()

    def base_tile(i, extra=None):
        w_copy(i).wait()
        part = jnp.dot(act_v[...], w_v[:, b_cols(i)], preferred_element_type=F32)
        if extra is not None:
            part = part + extra
        xb[mx, :, b_cols(i)] = part.astype(BF16)
        for p in range(1, t):
            xb_copy(i, p, mx).start()

    def early_take(j):
        if j == 0 or not trade:
            take(1, j)
        else:
            pl.when(jnp.logical_not(is_end))(lambda: take(1, j))

    others = tiles - span // tile
    for k in range(others):
        base_tile(order[k])
        early_take(k)

    if trade:

        @pl.when(is_end)
        def _():
            target = me + inward
            local_slot = slot_v[...] - target * voices
            chosen = (local_slot >= 0) & (local_slot < voices)
            ones = chosen.astype(F32)
            up_to = lax.broadcasted_iota(jnp.int32, (rows, rows), 0) <= lax.broadcasted_iota(
                jnp.int32, (rows, rows), 1
            )
            counted = jnp.dot(
                jnp.broadcast_to(ones, (8, rows)).astype(BF16),
                up_to.astype(F32).astype(BF16),
                preferred_element_type=F32,
            )[0:1]
            place = lax.broadcasted_iota(jnp.int32, (lanes, rows), 0).astype(F32) + 1.0
            perm = jnp.where((place == counted) & chosen, 1.0, 0.0)
            perm_v[...] = perm
            picked = perm.astype(BF16)
            rows_out[...] = jnp.dot(
                picked[: rows_out.shape[0]], act_v[...], preferred_element_type=F32
            ).astype(BF16)
            tag = jnp.where(chosen, local_slot + 1, 0).astype(F32)
            tags_out[...] = nt_dot(jnp.broadcast_to(tag, (8, rows)).astype(BF16), picked)
            tags_copy().start()
            rows_copy().start()

    wide0 = widen(me, rank_sum(0))
    per = span // tile
    for k in range(per):
        cols = pl.ds(k * tile, tile)
        base_tile(order[others + k], tn_dot(wide0, pu[mx, slab(me), cols]))
        if others + k < pieces:
            early_take(others + k)
    for j in range(tiles, pieces):
        early_take(j)
    total[...] = jnp.zeros_like(total)

    @pl.when(busy(1))
    def _():
        xr[1, mx] = jnp.zeros((rank, rows), F32)
        for j in range(1, pieces):
            process(1, j)
        send_rank(1)

    def serve():
        rows_copy().wait_recv()
        tags_copy().wait_recv()
        got = nt_dot(pd[me], rows_in[...])
        voice_of = (lax.broadcasted_iota(jnp.int32, (panel, lanes), 0) // rank).astype(F32)
        back_out[...] = fold(jnp.where(voice_of + 1.0 == tags_in[0:1], got, 0.0))
        back_copy().start()

    def step(s, carry):
        xr[s, mx] = jnp.zeros((rank, rows), F32)
        for j in range(pieces):
            take(s, j)
            if j > 1:
                process(s, j - 1)
            if trade and j == 2:
                pl.when(is_host & (s == 2))(serve)
        process(s, PARTS)
        if trade:

            @pl.when(is_end & (s == 2))
            def _():
                back_copy().wait_recv()
                xr[s, mx] += jnp.dot(
                    back_in[...],
                    perm_v[...],
                    precision=lax.Precision.HIGHEST,
                    preferred_element_type=F32,
                )

        pl.when(busy(s))(lambda: send_rank(s))
        pl.when(busy(s - 1))(lambda: settle(s - 1))
        return carry

    if trade:
        keep = lanes - rows_out.shape[0]
        if keep:
            rows_in[rows_out.shape[0] :] = jnp.zeros((keep, feat), BF16)
    lax.fori_loop(2, n, step, 0)

    def base_wait(i, carry):
        for p in range(1, t):
            xb_copy(i, p, peer(p)).wait_recv()
        acc = total[:, b_cols(i)]
        for x in range(t):
            acc = acc + xb[x, :, b_cols(i)].astype(F32)
        total[:, b_cols(i)] = acc
        for p in range(1, t):
            xb_copy(i, p, mx).wait_send()
        return carry

    lax.fori_loop(0, tiles, base_wait, 0)
    pl.when(busy(n - 1))(lambda: settle(n - 1))
    out[...] = total[...].astype(BF16)

    own_sends(range(pieces), lambda c: c.wait_send())
    for p in range(1, t):
        xr_copy(0, p, mx).wait_send()
    if trade:

        @pl.when(is_end)
        def _():
            rows_copy().wait_send()
            tags_copy().wait_send()

        pl.when(is_host)(lambda: back_copy().wait_send())

    def drain(s, carry):
        def sent(o, direction):
            for j in range(pieces):

                def one():
                    pl.when(on_line(me + direction))(lambda: z_copy(direction, o, j).wait_send())
                    sib_copy(o, j, core).wait_send()

                if j == 0 or not trade:
                    one()
                else:
                    pl.when(jnp.logical_not(is_end & (s == 1)))(one)
            for p in range(1, t):
                xu_copy(o, p).wait_send()
                xu_arrival(o, p, core, sx_send, sx_recv).wait_send()

        both(s, sent)

        @pl.when(busy(s))
        def _():
            for p in range(1, t):
                xr_copy(s, p, mx).wait_send()

        return carry

    lax.fori_loop(1, n, drain, 0)


def local(n, t, activations, row_voice, slot_table, weight, down, up):
    rows, feat = activations.shape
    voices, rank, span = up.shape
    width = weight.shape[1]
    panel = voices * rank
    tiles = width // min(TILE, span)
    cap = max(2, rows // min(n, 8))
    sent_rows = -(-cap // 16) * 16
    lanes = -(-cap // 128) * 128
    any_spec = pl.BlockSpec(memory_space=pl.ANY)
    dma = pltpu.SemaphoreType.DMA
    return pl.pallas_call(
        functools.partial(kernel, n, t, voices, rank, cap),
        out_shape=pltpu.VMEM((rows, width), BF16),
        in_specs=[
            pl.BlockSpec(memory_space=pltpu.VMEM),
            pl.BlockSpec(memory_space=pltpu.SMEM),
            any_spec,
            any_spec,
            any_spec,
            any_spec,
        ],
        out_specs=pl.BlockSpec(memory_space=pltpu.VMEM),
        scratch_shapes=[
            pltpu.VMEM((rows, feat), BF16),
            pltpu.VMEM((feat, width), BF16),
            pltpu.VMEM((n, panel, feat), BF16),
            pltpu.VMEM((t, n * panel, span), BF16),
            pltpu.VMEM((t, rows, width), BF16),
            pltpu.VMEM((rows, width), F32),
            pltpu.VMEM((n, t, rank, rows), F32),
            pltpu.VMEM((1, rows), jnp.int32),
            pltpu.VMEM((2, panel, rows), F32),
            pltpu.VMEM((lanes, rows), F32),
            pltpu.VMEM((sent_rows, feat), BF16),
            pltpu.VMEM((8, lanes), F32),
            pltpu.VMEM((lanes, feat), BF16),
            pltpu.VMEM((8, lanes), F32),
            pltpu.VMEM((rank, lanes), F32),
            pltpu.VMEM((rank, lanes), F32),
            dma((2, n, PARTS + 1)),
            dma((n, PARTS + 1)),
            dma((n, PARTS + 1)),
            dma((n, PARTS + 1)),
            dma((n, t)),
            dma((n, t)),
            dma((n, t)),
            dma((n, t)),
            dma((tiles, t)),
            dma((tiles, t)),
            dma((n, t)),
            dma((n, t)),
            dma((tiles,)),
            dma((3,)),
            dma((3,)),
            dma((3,)),
        ],
        compiler_params=pltpu.CompilerParams(
            collective_id=0, has_side_effects=True, vmem_limit_bytes=56 * 1024 * 1024
        ),
    )(
        row_voice,
        slot_table,
        activations,
        weight,
        down.reshape(panel, feat),
        up.reshape(panel, span),
    )


def solution(mesh):
    in_specs = (
        P(("groups", "replica", "sub"), "tensor"),
        P(("groups", "replica", "sub")),
        P("groups"),
        P("tensor", None),
        P(("groups", "replica"), None, "tensor"),
        P(("groups", "replica"), None, "tensor"),
    )
    out_specs = P(("groups", "replica", "sub"), None)
    body = functools.partial(local, mesh.shape["replica"], mesh.shape["tensor"])
    return jax.shard_map(body, mesh=mesh, in_specs=in_specs, out_specs=out_specs, check_vma=False)
```
